256 devices in a mesh: section: 4 (over x), tok: 64 (over y, z, core).
Axes of the slice: x: 4, y: 4, z: 8, core: 2. Of those that a mesh axis runs over, the one named last changes fastest.
Arguments:
- queries: bfloat16 [4, 8192, 5120], P('section', 'tok'), may hold values from -4 to 4
- keys: bfloat16 [4, 8192, 5120], P('section', 'tok'), may hold values from -12 to 12
- values: bfloat16 [4, 8192, 5120], P('section', 'tok'), may hold values from -4 to 4
- cluster_ids: int32 [4, 8192, 2], P('section', 'tok'), may hold values from 0 to 63, as said below
Outputs:
- handed: bfloat16 [4, 8192, 5120], P('section', 'tok')
The draws below stay inside these ranges and needn't reach their ends.
Inputs may be any that keep to these rules, and one draw needn't show every extreme that they name: `cluster_ids`: each token names two different clusters. Among the 128 tokens of one index of tok no cluster is named more than 8 times; in every section one cluster is named exactly 8 times by the tokens of every index of tok, and one cluster by none of them.
All inputs are finite; a program needn't handle non-finite values.
Results may differ from the reference program's by a relative error of at most 0.0051.
Values may be sent and summed in bfloat16 or wider, within the bound.
A program may use at most 64 MiB of HBM per device.

```python
import math
import jax
import jax.numpy as jnp
from jax import lax

HD = 128
TOK_DEV = 128
WIN = 128
BLOCK = 256
D = 5120
SECTIONS = 4
SEQ = 8192
CLUSTERS = 64
MOST = 8
CAPACITY = 512


def section_picks(section_key):
    base_count = MOST // 2
    pair_count = CLUSTERS // 2
    key_perm, key_gap, key_dev = jax.random.split(section_key, 3)
    cluster_order = jax.random.permutation(key_perm, CLUSTERS).astype(jnp.int32)
    spread = jax.random.randint(key_gap, (pair_count,), 0, base_count - 1, dtype=jnp.int32)
    spread = spread.at[0].set(base_count)
    paired = jnp.stack([base_count + spread, base_count - spread], axis=1).reshape(-1)

    def device_picks(dev_key):
        key_mix, key_jit, key_pos = jax.random.split(dev_key, 3)
        others = jax.random.permutation(key_mix, CLUSTERS - 2).astype(jnp.int32) + 2
        jitter = jax.random.randint(key_jit, (pair_count - 1,), 0, 2, dtype=jnp.int32)
        shifts = jnp.stack([jitter, -jitter], axis=1).reshape(-1)
        ordered = paired.at[others].add(shifts)
        counts = jnp.zeros((CLUSTERS,), jnp.int32).at[cluster_order].set(ordered)
        run_ends = jnp.cumsum(counts, dtype=jnp.int32)
        labels = jnp.sum((jnp.arange(2 * TOK_DEV, dtype=jnp.int32)[:, None] >= run_ends[None, :]).astype(jnp.int32), axis=1)
        pair_order = jax.random.permutation(key_pos, TOK_DEV // 2).astype(jnp.int32)
        places = (2 * pair_order[:, None] + jnp.arange(2, dtype=jnp.int32)[None, :]).reshape(-1)
        return jnp.stack([labels[places], labels[places + TOK_DEV]], axis=1)
    dev_keys = jax.random.split(key_dev, CLUSTERS)
    return jax.vmap(device_picks)(dev_keys).reshape(SEQ, 2)


def draw_cluster_ids(key, part):
    section_keys = jax.random.split(jax.random.fold_in(key, 11), SECTIONS)
    return jax.vmap(section_picks)(section_keys).astype(jnp.int32)


def draw_queries(key, part):
    drawn = jnp.clip(jax.random.normal(jax.random.fold_in(key, 3), (SECTIONS, SEQ, D), jnp.float32), -4.0, 4.0)
    return drawn.astype(jnp.bfloat16)


def draw_keys(key, part):
    drawn = jnp.clip(jax.random.normal(jax.random.fold_in(key, 5), (SECTIONS, SEQ, D), jnp.float32), -4.0, 4.0)
    return drawn.astype(jnp.bfloat16)


def block_scale(key, shape, cuts, low, high):
    loudness, own = 1.0, jax.random.fold_in(key, 6)
    for position, parts in cuts:
        heights = jnp.exp(jax.random.uniform(jax.random.fold_in(own, position), (parts,), jnp.float32, low / len(cuts), high / len(cuts)))
        loudness = loudness * jnp.repeat(heights, shape[position] // parts).reshape([-1 if axis == position else 1 for axis in range(len(shape))])
    return loudness


def scatter_about(rng, extent, deviation, bound, shards=(), kind=jnp.bfloat16):
    result = jax.random.normal(rng, extent, jnp.float32) * deviation
    if len(shards) > 0:
        result = block_scale(rng, extent, shards, -0.22, 0.18) * result
    return jnp.clip(result, min=-bound, max=bound).astype(kind)


def setup_inputs(seed: int = 0) -> dict:
    key_of = jax.random.split(jax.random.key(seed), 5)
    queries = draw_queries(jax.random.fold_in(key_of[4], 71), 0)
    keys = draw_keys(jax.random.fold_in(key_of[4], 71), 0)
    values = scatter_about(key_of[2], (SECTIONS, SEQ, D), 1.0, 4.0, ((0, 4), (1, 64)))
    cluster_ids = draw_cluster_ids(jax.random.fold_in(key_of[4], 71), 0)
    return dict(queries=queries, keys=keys, values=values, cluster_ids=cluster_ids)


def softmax_mix(query_blk, key_blk, value_blk, allowed):
    score_scale = 1.0 / math.sqrt(HD)
    scores = jnp.einsum('bqhe,bkhe->bhqk', query_blk.astype(jnp.float32), key_blk.astype(jnp.float32)) * score_scale
    scores = jnp.where(allowed[:, None], scores, -1e+30)
    highest = lax.optimization_barrier(jnp.max(scores, axis=-1, keepdims=True))
    weights = jnp.exp(scores - highest)
    weight_sum = lax.optimization_barrier(jnp.sum(weights, axis=-1))
    rounded = lax.optimization_barrier(weights.astype(jnp.bfloat16)).astype(jnp.float32)
    mixed = jnp.einsum('bhqk,bkhe->bqhe', rounded, value_blk.astype(jnp.float32))
    return mixed / jnp.transpose(weight_sum, (0, 2, 1))[..., None]

def window_mix(query_loc, key_all, value_all, block_base):
    window_len = key_all.shape[0] - query_loc.shape[0]
    blocks = query_loc.shape[0] // window_len
    heads_here = query_loc.shape[1] // HD
    query_blk = query_loc.reshape(blocks, window_len, heads_here, HD)
    key_blk = jnp.concatenate([key_all[:-window_len].reshape(blocks, window_len, heads_here, HD), key_all[window_len:].reshape(blocks, window_len, heads_here, HD)], axis=1)
    value_blk = jnp.concatenate([value_all[:-window_len].reshape(blocks, window_len, heads_here, HD), value_all[window_len:].reshape(blocks, window_len, heads_here, HD)], axis=1)
    rows_at = jnp.arange(window_len, dtype=jnp.int32)[:, None]
    cols_at = jnp.arange(2 * window_len, dtype=jnp.int32)[None, :]
    inside = (cols_at > rows_at) & (cols_at <= rows_at + window_len)
    opening = block_base + jnp.arange(blocks, dtype=jnp.int32) == 0
    allowed = inside[None] & (jnp.logical_not(opening)[:, None, None] | (cols_at >= window_len)[None])
    return softmax_mix(query_blk, key_blk, value_blk, allowed).reshape(query_loc.shape).astype(jnp.bfloat16)

def local_part(query_loc, key_loc, value_loc):
    groups = SEQ // TOK_DEV
    pad_rows = jnp.zeros((WIN, key_loc.shape[1]), key_loc.dtype)
    key_pad = jnp.concatenate([pad_rows, key_loc], axis=0)
    value_pad = jnp.concatenate([pad_rows, value_loc], axis=0)

    def one_group(group):
        start = (group * TOK_DEV).astype(jnp.int32)
        query_part = lax.dynamic_slice_in_dim(query_loc, start, TOK_DEV, 0)
        key_part = lax.dynamic_slice_in_dim(key_pad, start, TOK_DEV + WIN, 0)
        value_part = lax.dynamic_slice_in_dim(value_pad, start, TOK_DEV + WIN, 0)
        return window_mix(query_part, key_part, value_part, group * (TOK_DEV // WIN))
    return lax.map(one_group, jnp.arange(groups, dtype=jnp.int32)).reshape(SEQ, -1)

def route_part(route_query, route_key, route_value, cluster_pick):
    half_width = route_query.shape[1]
    route_heads = half_width // HD
    blocks = CAPACITY // BLOCK
    member = lax.optimization_barrier(jnp.sum((cluster_pick[:, :, None] == jnp.arange(CLUSTERS, dtype=jnp.int32)[None, None, :]).astype(jnp.int32), axis=1))
    inclusive = jnp.cumsum(member, axis=0, dtype=jnp.int32)
    pick_rank = (jnp.take_along_axis(inclusive, cluster_pick, axis=1) - 1).astype(jnp.int32)
    token_index = jnp.broadcast_to(jnp.arange(SEQ, dtype=jnp.int32)[:, None], (SEQ, 2))
    slot_token = jnp.full((CLUSTERS, CAPACITY), SEQ, jnp.int32).at[cluster_pick, pick_rank].set(token_index)
    places = jnp.arange(BLOCK, dtype=jnp.int32)
    causal = places[None, :] <= places[:, None]
    diagonal = places[None, :] == places[:, None]

    def one_cluster(row_tokens):
        filled = row_tokens < SEQ
        safe_row = jnp.minimum(row_tokens, SEQ - 1)
        query_blk = route_query[safe_row].reshape(blocks, BLOCK, route_heads, HD)
        key_blk = route_key[safe_row].reshape(blocks, BLOCK, route_heads, HD)
        value_blk = route_value[safe_row].reshape(blocks, BLOCK, route_heads, HD)
        allowed = causal[None] & (filled.reshape(blocks, 1, BLOCK) | diagonal[None])
        return softmax_mix(query_blk, key_blk, value_blk, allowed).reshape(CAPACITY, half_width).astype(jnp.bfloat16)
    routed = lax.map(one_cluster, slot_token)
    gathered = routed[cluster_pick, pick_rank]
    return (gathered[:, 0].astype(jnp.float32) + gathered[:, 1].astype(jnp.float32)).astype(jnp.bfloat16)

def section_layer(operands):
    section_query, section_key, section_value, cluster_pick = operands
    half_width = section_query.shape[1] // 2
    local_out = local_part(section_query[:, :half_width], section_key[:, :half_width], section_value[:, :half_width])
    route_out = route_part(section_query[:, half_width:], section_key[:, half_width:], section_value[:, half_width:], cluster_pick)
    return jnp.concatenate([local_out, route_out], axis=1)

def reference(queries, keys, values, cluster_ids):
    layers = lax.map(section_layer, (queries, keys, values, cluster_ids))
    return jnp.roll(layers, 1, axis=0)
```

```python
import functools
import math

import jax
import jax.numpy as jnp
from jax import lax
from jax.experimental import pallas as pl
from jax.experimental.pallas import tpu as pltpu
from jax.sharding import PartitionSpec as P

HD = 128
TOK = 128
HEADS = 20
HALF = HEADS * HD
PEERS = 64
CLUSTERS = 64
MOST = 8
SLOTS = PEERS * MOST
BLOCK = 256
LOW = -1e30
SCALE = math.log2(math.e) / math.sqrt(HD)
MESH = pl.DeviceIdType.MESH
BF16 = jnp.bfloat16
F32 = jnp.float32


def owner_of(head):
    pair = head // 5
    within = head % 5
    z = pair * 2 + within // 3
    y = head % 4
    return (y * 8 + z) * 2


def iota(shape, dim):
    return lax.broadcasted_iota(jnp.int32, shape, dim)


def dot(a, b, dims=((1,), (0,))):
    return lax.dot_general(a, b, (dims, ((), ())), preferred_element_type=F32)


def one_hot(hit):
    return jnp.where(hit, 1.0, 0.0).astype(BF16)


def layer_kernel(
    query, key, value, ids, out,
    meta, slots, qkbuf, vbuf, qe, ke, ve, bias0, bias1, split,
    lq, lk, lv, tails, lout,
    meta_send, meta_recv, bulk_send, qk_recv, v_recv, tail_send, tail_recv,
    load_sem, lout_send, back_send, out_recv, ready,
):
    s = lax.axis_index("section")
    t = lax.axis_index("tok")
    y, z, core = t // 16, (t // 2) % 8, t % 2
    first = (z // 2) * 5 + (z % 2) * 3
    offset = (y - first + 64) % 4
    head = first + offset
    is_owner = jnp.logical_and(offset < 3 - z % 2, core == 0)
    next_t, prev_t = (t + 1) % PEERS, (t + PEERS - 1) % PEERS
    next_s, prev_s = (s + 1) % 4, (s + 3) % 4

    barrier = pltpu.get_barrier_semaphore()

    @pl.when(is_owner)
    def _():
        @pl.loop(1, PEERS)
        def _(j):
            pl.semaphore_signal(
                barrier, inc=1, device_id=(s, (t + j) % PEERS), device_id_type=MESH
            )

    for peer in ((s, prev_t), (prev_s, t), (next_s, t)):
        pl.semaphore_signal(barrier, inc=1, device_id=peer, device_id_type=MESH)

    slots[...] = jnp.zeros_like(slots)
    col0, col1 = ids[:, 0:1], ids[:, 1:2]
    rows_at, cols_at = iota((TOK, TOK), 0), iota((TOK, TOK), 1)
    eye = rows_at == cols_at
    earlier = rows_at < cols_at
    for j, col in enumerate((col0, col1)):
        row = jnp.sum(jnp.where(eye, col, 0), axis=0, keepdims=True)
        same = jnp.logical_and(earlier, jnp.logical_or(col0 == row, col1 == row))
        rank = jnp.sum(jnp.where(same, 1, 0), axis=0, keepdims=True)
        slots[j : j + 1, :] = row * MOST + rank
    named = jnp.logical_or(col0 == cols_at, col1 == cols_at)
    slots[2:3, :] = jnp.sum(jnp.where(named, 1, 0), axis=0, keepdims=True)

    loads = [
        pltpu.make_async_copy(src.at[:, pl.ds(0, HALF)], dst, load_sem.at[a])
        for a, (src, dst) in enumerate(((query, lq), (key, lk), (value, lv)))
    ]
    for load in loads:
        load.start()

    pl.semaphore_wait(barrier, jnp.where(is_owner, HEADS - 1, HEADS) + 3)

    def spread(source, target, send, recv):
        @pl.loop(0, HEADS)
        def _(i):
            h = (i + first + core * 10) % HEADS
            owner = owner_of(h)

            @pl.when(owner != t)
            def _():
                pltpu.make_async_remote_copy(
                    src_ref=source(h), dst_ref=target, send_sem=send, recv_sem=recv,
                    device_id=(s, owner), device_id_type=MESH,
                ).start()

            @pl.when(owner == t)
            def _():
                pltpu.make_async_copy(source(h), target, recv).start()

    def head_block(array):
        return lambda h: array.at[:, pl.ds(pl.multiple_of(HALF + h * HD, HD), HD)]

    spread(lambda h: slots, meta.at[t], meta_send, meta_recv)
    tail_copies = [
        pltpu.make_async_remote_copy(
            src_ref=src.at[:, pl.ds(0, HALF)], dst_ref=tails.at[a],
            send_sem=tail_send.at[a], recv_sem=tail_recv.at[a],
            device_id=(s, next_t), device_id_type=MESH,
        )
        for a, src in enumerate((key, value))
    ]
    for copy in tail_copies:
        copy.start()
    spread(head_block(query), qkbuf.at[t, :, pl.ds(0, HD)], bulk_send.at[0], qk_recv)
    spread(head_block(key), qkbuf.at[t, :, pl.ds(HD, HD)], bulk_send.at[1], qk_recv)
    spread(head_block(value), vbuf.at[t], bulk_send.at[2], v_recv)

    @pl.when(is_owner)
    def _():
        pltpu.make_async_copy(meta, meta, meta_recv).wait()
        counts = meta[:, 2, :].astype(F32).astype(BF16)
        dev = iota((PEERS, SLOTS), 0)
        of_dev = iota((PEERS, SLOTS), 1) // MOST
        count = dot(counts, one_hot(dev == of_dev), ((0,), (0,)))
        before = dot(counts, one_hot(dev < of_dev), ((0,), (0,)))
        place = (iota((TOK, SLOTS), 1) % MOST).astype(F32)
        filled = place < count
        second = before + jnp.minimum(place, count) >= BLOCK
        bias0[...] = jnp.where(filled, 0.0, LOW)
        bias1[...] = jnp.where(jnp.logical_and(filled, second), 0.0, LOW)
        start = jnp.sum(jnp.where(second, 0.0, 1.0), axis=1, keepdims=True)
        split[...] = jnp.broadcast_to(start, (TOK, TOK))

    for load in loads:
        load.wait()
    for copy in tail_copies:
        copy.wait()

    @pl.loop(0, HEADS)
    def _(h):
        at = pl.ds(pl.multiple_of(h * HD, HD), HD)
        q_h = lq[:, at]
        before = dot(q_h, tails[0, :, at], ((1,), (1,))) * SCALE
        own = dot(q_h, lk[:, at], ((1,), (1,))) * SCALE
        reach = jnp.where(t == 0, TOK, 0)
        before = jnp.where(cols_at > rows_at + reach, before, LOW)
        own = jnp.where(cols_at <= rows_at, own, LOW)
        top = jnp.maximum(
            jnp.max(before, axis=1, keepdims=True), jnp.max(own, axis=1, keepdims=True)
        )
        before, own = jnp.exp2(before - top), jnp.exp2(own - top)
        total = jnp.sum(before + own, axis=1, keepdims=True)
        mixed = dot(before.astype(BF16), tails[1, :, at]) + dot(own.astype(BF16), lv[:, at])
        lout[:, at] = (mixed / total).astype(BF16)

    local_copy = pltpu.make_async_remote_copy(
        src_ref=lout, dst_ref=out.at[:, pl.ds(0, HALF)], send_sem=lout_send, recv_sem=out_recv,
        device_id=(next_s, t), device_id_type=MESH,
    )
    local_copy.start()

    @pl.when(is_owner)
    def _():
        slot_at = iota((SLOTS, TOK), 0)

        def members(d):
            return one_hot(
                jnp.logical_or(slot_at == meta[d, 0:1, :], slot_at == meta[d, 1:2, :])
            )

        def paired(a, b):
            width = a.shape[1]
            return jnp.concatenate(
                [a.reshape(CLUSTERS, MOST, width), b.reshape(CLUSTERS, MOST, width)], axis=1
            ).astype(BF16)

        pltpu.make_async_copy(qkbuf, qkbuf, qk_recv).wait()
        pl.semaphore_signal(ready, inc=1, device_id=(prev_s, t), device_id_type=MESH)

        @pl.loop(0, PEERS // 2)
        def _(i):
            at = pl.ds(pl.multiple_of(i * 2 * MOST, 2 * MOST), 2 * MOST)
            both = paired(dot(members(2 * i), qkbuf[2 * i]), dot(members(2 * i + 1), qkbuf[2 * i + 1]))
            qe[:, at, :] = both[:, :, :HD]
            ke[:, at, :] = both[:, :, HD:]

        pltpu.make_async_copy(vbuf, vbuf, v_recv).wait()

        @pl.loop(0, PEERS // 2)
        def _(i):
            at = pl.ds(pl.multiple_of(i * 2 * MOST, 2 * MOST), 2 * MOST)
            ve[:, at, :] = paired(dot(members(2 * i), vbuf[2 * i]), dot(members(2 * i + 1), vbuf[2 * i + 1]))

        pl.semaphore_wait(ready, 1)
        wide_at = iota((TOK, 2 * SLOTS), 1)
        for part in range(SLOTS // TOK):
            reach = (part + 1) * TOK

            @pl.loop(0, CLUSTERS)
            def _(c):
                q_c = qe[c, part * TOK : reach, :]
                scores = dot(q_c, ke[c, 0:reach, :], ((1,), (1,))) * SCALE
                row0, row1 = bias0[pl.ds(c, 1), :], bias1[pl.ds(c, 1), :]
                later = rows_at.astype(F32) + part * TOK >= split[pl.ds(c, 1), :]
                tiles = []
                for j in range(part + 1):
                    cut = slice(j * TOK, (j + 1) * TOK)
                    if part < BLOCK // TOK:
                        tile = scores[:, cut] + row0[:, cut]
                    else:
                        tile = scores[:, cut] + jnp.where(later, row1[:, cut], row0[:, cut])
                    if j == part:
                        tile = jnp.where(cols_at <= rows_at, tile, LOW)
                    tiles.append(tile)
                top = jnp.max(functools.reduce(jnp.maximum, tiles), axis=1, keepdims=True)
                tiles = [jnp.exp2(tile - top) for tile in tiles]
                total = jnp.sum(functools.reduce(jnp.add, tiles), axis=1, keepdims=True)
                weights = jnp.concatenate([tile.astype(BF16) for tile in tiles], axis=1)
                mixed = dot(weights, ve[c, 0:reach, :])
                qe[c, part * TOK : reach, :] = (mixed / total).astype(BF16)

            @pl.loop(part * 8, part * 8 + 8)
            def _(i):
                at = pl.ds(pl.multiple_of(i * 2 * MOST, 2 * MOST), 2 * MOST)
                rows = qe[:, at, :].reshape(2 * SLOTS, HD)
                for side in range(2):
                    d = 2 * i + side
                    hits = []
                    for j in range(2):
                        slot = meta[d, j : j + 1, :]
                        wide = (slot // MOST) * (2 * MOST) + slot % MOST + side * MOST
                        col = jnp.sum(jnp.where(eye, wide, 0), axis=1, keepdims=True)
                        hits.append(wide_at == col)
                    vbuf[d] = dot(one_hot(jnp.logical_or(*hits)), rows).astype(BF16)
                    pltpu.make_async_remote_copy(
                        src_ref=vbuf.at[d],
                        dst_ref=out.at[:, pl.ds(pl.multiple_of(HALF + head * HD, HD), HD)],
                        send_sem=back_send, recv_sem=out_recv,
                        device_id=(next_s, d), device_id_type=MESH,
                    ).start()

        pltpu.make_async_copy(vbuf, vbuf, back_send).wait()

    local_copy.wait_send()
    for sem, one in ((meta_send, None), (bulk_send.at[0], 0), (bulk_send.at[1], 0), (bulk_send.at[2], 0)):
        for many, mine in ((HEADS - 1, True), (HEADS, False)):
            @pl.when(is_owner if mine else jnp.logical_not(is_owner))
            def _():
                ref = meta.at[pl.ds(0, many)] if one is None else vbuf.at[pl.ds(0, many)]
                pltpu.make_async_copy(ref, ref, sem).wait()
    pltpu.make_async_copy(out, out, out_recv).wait()


def on_device(queries, keys, values, cluster_ids):
    any_space = pl.BlockSpec(memory_space=pl.ANY)
    vmem = pltpu.VMEM
    expanded = vmem((CLUSTERS, SLOTS, HD), BF16)
    wide = vmem((TOK, HALF), BF16)
    dma = pltpu.SemaphoreType.DMA
    layer = pl.pallas_call(
        layer_kernel,
        out_shape=jax.ShapeDtypeStruct((TOK, 2 * HALF), BF16),
        in_specs=[any_space] * 3 + [pl.BlockSpec(memory_space=vmem)],
        out_specs=any_space,
        scratch_shapes=[
            vmem((PEERS, 8, TOK), jnp.int32),
            vmem((8, TOK), jnp.int32),
            vmem((PEERS, TOK, 2 * HD), BF16),
            vmem((PEERS, TOK, HD), BF16),
            expanded, expanded, expanded,
            vmem((TOK, SLOTS), F32),
            vmem((TOK, SLOTS), F32),
            vmem((TOK, TOK), F32),
            wide, wide, wide,
            vmem((2, TOK, HALF), BF16),
            wide,
            dma, dma, dma((3,)), dma, dma, dma((2,)), dma((2,)),
            dma((3,)), dma, dma, dma, pltpu.SemaphoreType.REGULAR,
        ],
        compiler_params=pltpu.CompilerParams(
            collective_id=0, has_side_effects=True, vmem_limit_bytes=60 << 20
        ),
    )(queries[0], keys[0], values[0], cluster_ids[0])
    return layer[None]


def solution(mesh):
    spec = P("section", "tok", None)
    return jax.shard_map(
        on_device, mesh=mesh, in_specs=(spec,) * 4, out_specs=spec, check_vma=False
    )
```

```python
import functools
import math

import jax
import jax.numpy as jnp
from jax import lax
from jax.experimental import pallas as pl
from jax.experimental.pallas import tpu as pltpu
from jax.sharding import PartitionSpec as P

HD = 128
TOK = 128
HEADS = 20
HALF = HEADS * HD
PEERS = 64
CLUSTERS = 64
MOST = 8
GROUP = 8
LOCAL_GROUP = 5
SLOTS = PEERS * MOST
BLOCK = 256
LOW = -1e30
SCALE = math.log2(math.e) / math.sqrt(HD)
MESH = pl.DeviceIdType.MESH
BF16 = jnp.bfloat16
F32 = jnp.float32


def owner_of(head):
    pair = head // 5
    within = head % 5
    z = pair * 2 + within // 3
    y = head % 4
    return (y * 8 + z) * 2


def iota(shape, dim):
    return lax.broadcasted_iota(jnp.int32, shape, dim)


def dot(a, b, dims=((1,), (0,))):
    return lax.dot_general(a, b, (dims, ((), ())), preferred_element_type=F32)


def one_hot(hit):
    return jnp.where(hit, 1.0, 0.0).astype(BF16)


def layer_kernel(
    query, key, value, ids, out,
    meta, slots, qkbuf, vbuf, hot, qe, ke, ve, bias0, bias1, split,
    lq, lk, lv, tails, lout,
    meta_send, meta_recv, bulk_send, qk_recv, v_recv, tail_send, tail_recv,
    load_sem, lout_send, back_send, out_recv, ready,
):
    s = lax.axis_index("section")
    t = lax.axis_index("tok")
    y, z, core = t // 16, (t // 2) % 8, t % 2
    first = (z // 2) * 5 + (z % 2) * 3
    offset = (y - first + 64) % 4
    head = first + offset
    is_owner = jnp.logical_and(offset < 3 - z % 2, core == 0)
    next_t, prev_t = (t + 1) % PEERS, (t + PEERS - 1) % PEERS
    next_s, prev_s = (s + 1) % 4, (s + 3) % 4

    barrier = pltpu.get_barrier_semaphore()

    @pl.when(is_owner)
    def _():
        @pl.loop(1, PEERS)
        def _(j):
            pl.semaphore_signal(
                barrier, inc=1, device_id=(s, (t + j) % PEERS), device_id_type=MESH
            )

    for peer in ((s, prev_t), (prev_s, t), (next_s, t)):
        pl.semaphore_signal(barrier, inc=1, device_id=peer, device_id_type=MESH)

    slots[...] = jnp.zeros_like(slots)
    col0, col1 = ids[:, 0:1], ids[:, 1:2]
    rows_at, cols_at = iota((TOK, TOK), 0), iota((TOK, TOK), 1)
    eye = rows_at == cols_at
    earlier = rows_at < cols_at
    for j, col in enumerate((col0, col1)):
        row = jnp.sum(jnp.where(eye, col, 0), axis=0, keepdims=True)
        same = jnp.logical_and(earlier, jnp.logical_or(col0 == row, col1 == row))
        rank = jnp.sum(jnp.where(same, 1, 0), axis=0, keepdims=True)
        slots[j : j + 1, :] = row * MOST + rank
    named = jnp.logical_or(col0 == cols_at, col1 == cols_at)
    slots[2:3, :] = jnp.sum(jnp.where(named, 1, 0), axis=0, keepdims=True)

    loads = [
        pltpu.make_async_copy(src.at[:, pl.ds(0, HALF)], dst, load_sem.at[a])
        for a, (src, dst) in enumerate(((query, lq), (key, lk), (value, lv)))
    ]
    for load in loads:
        load.start()

    pl.semaphore_wait(barrier, jnp.where(is_owner, HEADS - 1, HEADS) + 3)

    def spread(source, target, send, recv):
        @pl.loop(0, HEADS)
        def _(i):
            h = (i + first + core * 10) % HEADS
            owner = owner_of(h)

            @pl.when(owner != t)
            def _():
                pltpu.make_async_remote_copy(
                    src_ref=source(h), dst_ref=target, send_sem=send, recv_sem=recv,
                    device_id=(s, owner), device_id_type=MESH,
                ).start()

            @pl.when(owner == t)
            def _():
                pltpu.make_async_copy(source(h), target, recv).start()

    def head_block(array):
        return lambda h: array.at[:, pl.ds(pl.multiple_of(HALF + h * HD, HD), HD)]

    spread(lambda h: slots, meta.at[t], meta_send, meta_recv)
    tail_copies = [
        pltpu.make_async_remote_copy(
            src_ref=src.at[:, pl.ds(0, HALF)], dst_ref=tails.at[a],
            send_sem=tail_send.at[a], recv_sem=tail_recv.at[a],
            device_id=(s, next_t), device_id_type=MESH,
        )
        for a, src in enumerate((key, value))
    ]
    for copy in tail_copies:
        copy.start()
    spread(head_block(query), qkbuf.at[t, :, pl.ds(0, HD)], bulk_send.at[0], qk_recv)
    spread(head_block(key), qkbuf.at[t, :, pl.ds(HD, HD)], bulk_send.at[1], qk_recv)
    spread(head_block(value), vbuf.at[t], bulk_send.at[2], v_recv)

    @pl.when(is_owner)
    def _():
        pltpu.make_async_copy(meta, meta, meta_recv).wait()
        counts = meta[:, 2, :].astype(F32).astype(BF16)
        dev = iota((PEERS, SLOTS), 0)
        of_dev = iota((PEERS, SLOTS), 1) // MOST
        count = dot(counts, one_hot(dev == of_dev), ((0,), (0,)))
        before = dot(counts, one_hot(dev < of_dev), ((0,), (0,)))
        place = (iota((TOK, SLOTS), 1) % MOST).astype(F32)
        filled = place < count
        second = before + jnp.minimum(place, count) >= BLOCK
        def by_cluster(array):
            return array[:CLUSTERS].reshape(CLUSTERS, 1, array.shape[1])

        bias0[...] = by_cluster(jnp.where(filled, 0.0, LOW))
        bias1[...] = by_cluster(jnp.where(jnp.logical_and(filled, second), 0.0, LOW))
        start = jnp.sum(jnp.where(second, 0.0, 1.0), axis=1, keepdims=True)
        split[...] = by_cluster(jnp.broadcast_to(start, (TOK, TOK)))

    for load in loads:
        load.wait()
    for copy in tail_copies:
        copy.wait()

    reach = jnp.where(t == 0, TOK, 0)
    window = cols_at > rows_at + reach
    causal = cols_at <= rows_at

    @pl.loop(0, HEADS // LOCAL_GROUP)
    def _(g):
        ats = [
            pl.ds(pl.multiple_of((g * LOCAL_GROUP + i) * HD, HD), HD) for i in range(LOCAL_GROUP)
        ]
        scores = [
            (dot(lq[:, at], tails[0, :, at], ((1,), (1,))), dot(lq[:, at], lk[:, at], ((1,), (1,))))
            for at in ats
        ]
        parts = []
        for before, own in scores:
            before = jnp.where(window, before * SCALE, LOW)
            own = jnp.where(causal, own * SCALE, LOW)
            top = jnp.max(jnp.maximum(before, own), axis=1, keepdims=True)
            before, own = jnp.exp2(before - top), jnp.exp2(own - top)
            total = jnp.sum(before + own, axis=1, keepdims=True)
            parts.append((before.astype(BF16), own.astype(BF16), total))
        mixed = [
            (dot(before, tails[1, :, at]) + dot(own, lv[:, at])) / total
            for at, (before, own, total) in zip(ats, parts)
        ]
        for at, mix in zip(ats, mixed):
            lout[:, at] = mix.astype(BF16)

    local_copy = pltpu.make_async_remote_copy(
        src_ref=lout, dst_ref=out.at[:, pl.ds(0, HALF)], send_sem=lout_send, recv_sem=out_recv,
        device_id=(next_s, t), device_id_type=MESH,
    )
    local_copy.start()

    @pl.when(is_owner)
    def _():
        slot_at = iota((SLOTS, TOK), 0)

        def members(d):
            return one_hot(
                jnp.logical_or(slot_at == meta[d, 0:1, :], slot_at == meta[d, 1:2, :])
            )

        def paired(a, b):
            width = a.shape[1]
            return jnp.concatenate(
                [a.reshape(CLUSTERS, MOST, width), b.reshape(CLUSTERS, MOST, width)], axis=1
            ).astype(BF16)

        pltpu.make_async_copy(qkbuf, qkbuf, qk_recv).wait()
        pl.semaphore_signal(ready, inc=1, device_id=(prev_s, t), device_id_type=MESH)

        def pair_at(i):
            return pl.ds(pl.multiple_of(i * 2 * MOST, 2 * MOST), 2 * MOST)

        @pl.loop(0, PEERS // 4)
        def _(g):
            products = []
            for i in range(4):
                hits = members(g * 4 + i)
                hot[g * 4 + i] = hits
                products.append(dot(hits, qkbuf[g * 4 + i]))
            for i in range(2):
                both = paired(products[2 * i], products[2 * i + 1])
                qe[:, pair_at(g * 2 + i), :] = both[:, :, :HD]
                ke[:, pair_at(g * 2 + i), :] = both[:, :, HD:]

        pltpu.make_async_copy(vbuf, vbuf, v_recv).wait()

        @pl.loop(0, PEERS // 8)
        def _(g):
            products = [dot(hot[g * 8 + i], vbuf[g * 8 + i]) for i in range(8)]
            for i in range(4):
                ve[:, pair_at(g * 4 + i), :] = paired(products[2 * i], products[2 * i + 1])

        pl.semaphore_wait(ready, 1)
        for part in range(SLOTS // TOK):
            lo, hi = part * TOK, (part + 1) * TOK

            def soften(scores, c):
                row0, row1 = bias0[c, :, :hi], bias1[c, :, :hi]
                later = rows_at.astype(F32) + lo >= split[c]
                tiles = []
                for j in range(part + 1):
                    cut = slice(j * TOK, (j + 1) * TOK)
                    bias = row0[:, cut]
                    if part >= BLOCK // TOK:
                        bias = jnp.where(later, row1[:, cut], bias)
                    tile = scores[:, cut] * SCALE + bias
                    if j == part:
                        tile = jnp.where(causal, tile, LOW)
                    tiles.append(tile)
                top = jnp.max(functools.reduce(jnp.maximum, tiles), axis=1, keepdims=True)
                tiles = [jnp.exp2(tile - top) for tile in tiles]
                total = jnp.sum(functools.reduce(jnp.add, tiles), axis=1, keepdims=True)
                return jnp.concatenate([tile.astype(BF16) for tile in tiles], axis=1), total

            @pl.loop(0, CLUSTERS // GROUP)
            def _(g):
                clusters = [g * GROUP + i for i in range(GROUP)]
                scores = [dot(qe[c, lo:hi, :], ke[c, 0:hi, :], ((1,), (1,))) for c in clusters]
                weights = [soften(score, c) for score, c in zip(scores, clusters)]
                mixed = [
                    (dot(weight, ve[c, 0:hi, :]) / total).astype(BF16)
                    for (weight, total), c in zip(weights, clusters)
                ]
                for c, mix in zip(clusters, mixed):
                    qe[c, lo:hi, :] = mix

            @pl.loop(part * 2, part * 2 + 2)
            def _(g):
                sums = []
                for i in range(4):
                    rows = qe[:, pair_at(g * 4 + i), :].astype(F32)
                    for side in range(2):
                        slot_rows = rows[:, side * MOST : (side + 1) * MOST, :]
                        slot_rows = slot_rows.reshape(SLOTS, HD).astype(BF16)
                        sums.append(dot(hot[g * 8 + 2 * i + side], slot_rows, ((0,), (0,))).astype(BF16))
                for i in range(8):
                    vbuf[g * 8 + i] = sums[i]
                for i in range(8):
                    pltpu.make_async_remote_copy(
                        src_ref=vbuf.at[g * 8 + i],
                        dst_ref=out.at[:, pl.ds(pl.multiple_of(HALF + head * HD, HD), HD)],
                        send_sem=back_send, recv_sem=out_recv,
                        device_id=(next_s, g * 8 + i), device_id_type=MESH,
                    ).start()

        pltpu.make_async_copy(vbuf, vbuf, back_send).wait()

    local_copy.wait_send()
    for sem, one in ((meta_send, None), (bulk_send.at[0], 0), (bulk_send.at[1], 0), (bulk_send.at[2], 0)):
        for many, mine in ((HEADS - 1, True), (HEADS, False)):
            @pl.when(is_owner if mine else jnp.logical_not(is_owner))
            def _():
                ref = meta.at[pl.ds(0, many)] if one is None else vbuf.at[pl.ds(0, many)]
                pltpu.make_async_copy(ref, ref, sem).wait()
    pltpu.make_async_copy(out, out, out_recv).wait()


def on_device(queries, keys, values, cluster_ids):
    any_space = pl.BlockSpec(memory_space=pl.ANY)
    vmem = pltpu.VMEM
    expanded = vmem((CLUSTERS, SLOTS, HD), BF16)
    wide = vmem((TOK, HALF), BF16)
    dma = pltpu.SemaphoreType.DMA
    layer = pl.pallas_call(
        layer_kernel,
        out_shape=jax.ShapeDtypeStruct((TOK, 2 * HALF), BF16),
        in_specs=[any_space] * 3 + [pl.BlockSpec(memory_space=vmem)],
        out_specs=any_space,
        scratch_shapes=[
            vmem((PEERS, 8, TOK), jnp.int32),
            vmem((8, TOK), jnp.int32),
            vmem((PEERS, TOK, 2 * HD), BF16),
            vmem((PEERS, TOK, HD), BF16),
            vmem((PEERS, SLOTS, TOK), BF16),
            expanded, expanded, expanded,
            vmem((CLUSTERS, 1, SLOTS), F32),
            vmem((CLUSTERS, 1, SLOTS), F32),
            vmem((CLUSTERS, 1, TOK), F32),
            wide, wide, wide,
            vmem((2, TOK, HALF), BF16),
            wide,
            dma, dma, dma((3,)), dma, dma, dma((2,)), dma((2,)),
            dma((3,)), dma, dma, dma, pltpu.SemaphoreType.REGULAR,
        ],
        compiler_params=pltpu.CompilerParams(
            collective_id=0, has_side_effects=True, vmem_limit_bytes=60 << 20
        ),
    )(queries[0], keys[0], values[0], cluster_ids[0])
    return layer[None]


def solution(mesh):
    spec = P("section", "tok", None)
    return jax.shard_map(
        on_device, mesh=mesh, in_specs=(spec,) * 4, out_specs=spec, check_vma=False
    )
```

```python
import functools
import math

import jax
import jax.numpy as jnp
from jax import lax
from jax.experimental import pallas as pl
from jax.experimental.pallas import tpu as pltpu
from jax.sharding import PartitionSpec as P

HD = 128
TOK = 128
HEADS = 20
HALF = HEADS * HD
PEERS = 64
CLUSTERS = 64
MOST = 8
LOCAL_GROUP = 5
EARLY = 10
SLOTS = PEERS * MOST
PARTS = SLOTS // TOK
GROUPS = (16, 16, 8, 8)
BLOCK = 256
LOW = -1e30
SCALE = math.log2(math.e) / math.sqrt(HD)
MESH = pl.DeviceIdType.MESH
BF16 = jnp.bfloat16
F32 = jnp.float32


def owner_of(head):
    pair = head // 5
    within = head % 5
    z = pair * 2 + within // 3
    y = head % 4
    return (y * 8 + z) * 2 + 1


def iota(shape, dim):
    return lax.broadcasted_iota(jnp.int32, shape, dim)


def dot(a, b, dims=((1,), (0,))):
    return lax.dot_general(a, b, (dims, ((), ())), preferred_element_type=F32)


def one_hot(hit):
    return jnp.where(hit, 1.0, 0.0).astype(BF16)


def layer_kernel(
    query, key, value, ids, out,
    meta, slots, qbuf, kbuf, vbuf, hot, qe, ke, weights0, weights1, weights2, weights3,
    bias0, bias1, split, lq, lk, lv, tails, lout,
    meta_send, meta_recv, bulk_send, q_recv, k_recv, v_recv, tail_send, tail_recv,
    load_sem, lout_send, back_send, out_recv, ready,
):
    s = lax.axis_index("section")
    t = lax.axis_index("tok")
    y, z, core = t // 16, (t // 2) % 8, t % 2
    first = (z // 2) * 5 + (z % 2) * 3
    offset = (y - first + 64) % 4
    head = first + offset
    is_owner = jnp.logical_and(offset < 3 - z % 2, core == 1)
    next_t, prev_t = (t + 1) % PEERS, (t + PEERS - 1) % PEERS
    next_s, prev_s = (s + 1) % 4, (s + 3) % 4

    barrier = pltpu.get_barrier_semaphore()

    @pl.when(is_owner)
    def _():
        @pl.loop(1, PEERS)
        def _(j):
            pl.semaphore_signal(
                barrier, inc=1, device_id=(s, (t + j) % PEERS), device_id_type=MESH
            )

    for peer in ((s, prev_t), (prev_s, t), (next_s, t)):
        pl.semaphore_signal(barrier, inc=1, device_id=peer, device_id_type=MESH)

    slots[...] = jnp.zeros_like(slots)
    rows_at, cols_at = iota((TOK, TOK), 0), iota((TOK, TOK), 1)
    eye = rows_at == cols_at
    earlier = rows_at < cols_at
    picks = [ids[j : j + 1, :] for j in range(2)]
    col0, col1 = [jnp.sum(jnp.where(eye, row, 0), axis=1, keepdims=True) for row in picks]
    for j, row in enumerate(picks):
        same = jnp.logical_and(earlier, jnp.logical_or(col0 == row, col1 == row))
        rank = jnp.sum(jnp.where(same, 1, 0), axis=0, keepdims=True)
        slots[j : j + 1, :] = row * MOST + rank
    named = jnp.logical_or(col0 == cols_at, col1 == cols_at)
    slots[2:3, :] = jnp.sum(jnp.where(named, 1, 0), axis=0, keepdims=True)

    loads = [
        pltpu.make_async_copy(src.at[:, pl.ds(0, HALF)], dst, load_sem.at[a])
        for a, (src, dst) in enumerate(((query, lq), (key, lk), (value, lv)))
    ]
    for load in loads:
        load.start()

    pl.semaphore_wait(barrier, jnp.where(is_owner, HEADS - 1, HEADS) + 3)

    def spread(source, target, send, recv):
        @pl.loop(0, HEADS)
        def _(i):
            step = jnp.where(i % 2 == 0, i // 2, HEADS - 1 - i // 2)
            h = (first + step) % HEADS
            owner = owner_of(h)

            @pl.when(owner != t)
            def _():
                pltpu.make_async_remote_copy(
                    src_ref=source(h), dst_ref=target, send_sem=send, recv_sem=recv,
                    device_id=(s, owner), device_id_type=MESH,
                ).start()

            @pl.when(owner == t)
            def _():
                pltpu.make_async_copy(source(h), target, recv).start()

    def head_block(array):
        return lambda h: array.at[:, pl.ds(pl.multiple_of(HALF + h * HD, HD), HD)]

    def columns(half):
        return pl.ds(half * EARLY * HD, (EARLY if half == 0 else HEADS - EARLY) * HD)

    def tail_copies(half):
        return [
            pltpu.make_async_remote_copy(
                src_ref=src.at[:, columns(half)], dst_ref=tails.at[a, :, columns(half)],
                send_sem=tail_send.at[half, a], recv_sem=tail_recv.at[half, a],
                device_id=(s, next_t), device_id_type=MESH,
            )
            for a, src in enumerate((key, value))
        ]

    def start_tails(half):
        for copy in tail_copies(half):
            copy.start()

    spread(lambda h: slots, meta.at[t], meta_send, meta_recv)
    start_tails(0)

    @pl.when(core == 0)
    def _():
        start_tails(1)

    spread(head_block(query), qbuf.at[t], bulk_send.at[0], q_recv.at[z])
    spread(head_block(key), kbuf.at[t], bulk_send.at[1], k_recv.at[z])

    def await_sends(sem, buf):
        for many, mine in ((HEADS - 1, True), (HEADS, False)):

            @pl.when(is_owner if mine else jnp.logical_not(is_owner))
            def _():
                ref = buf.at[pl.ds(0, many)]
                pltpu.make_async_copy(ref, ref, sem).wait()

    @pl.when(is_owner)
    def _():
        pltpu.make_async_copy(meta, meta, meta_recv).wait()
        counts = meta[:, 2, :].astype(F32).astype(BF16)
        dev = iota((PEERS, SLOTS), 0)
        of_dev = iota((PEERS, SLOTS), 1) // MOST
        count = dot(counts, one_hot(dev == of_dev), ((0,), (0,)))
        before = dot(counts, one_hot(dev < of_dev), ((0,), (0,)))
        place = (iota((TOK, SLOTS), 1) % MOST).astype(F32)
        filled = place < count
        second = before + jnp.minimum(place, count) >= BLOCK
        def by_cluster(array):
            return array[:CLUSTERS].reshape(CLUSTERS, 1, array.shape[1])

        slot_at = iota((SLOTS, TOK), 0)

        @pl.loop(0, PEERS // 4)
        def _(g):
            for i in range(4):
                d = g * 4 + i
                hot[d] = one_hot(
                    jnp.logical_or(slot_at == meta[d, 0:1, :], slot_at == meta[d, 1:2, :])
                )

        bias0[...] = by_cluster(jnp.where(filled, 0.0, LOW))
        bias1[...] = by_cluster(jnp.where(jnp.logical_and(filled, second), 0.0, LOW))
        start = jnp.sum(jnp.where(second, 0.0, 1.0), axis=1, keepdims=True)
        split[...] = by_cluster(jnp.broadcast_to(start, (TOK, TOK)))

    reach = jnp.where(t == 0, TOK, 0)
    window = cols_at > rows_at + reach
    causal = cols_at <= rows_at

    def local_copy(half):
        return pltpu.make_async_remote_copy(
            src_ref=lout.at[:, columns(half)], dst_ref=out.at[:, columns(half)],
            send_sem=lout_send.at[half], recv_sem=out_recv,
            device_id=(next_s, t), device_id_type=MESH,
        )

    def local_heads(half):
        for copy in tail_copies(half):
            copy.wait_recv()
        lo, hi = (0, EARLY) if half == 0 else (EARLY, HEADS)

        @pl.loop(lo // LOCAL_GROUP, hi // LOCAL_GROUP)
        def _(g):
            ats = [
                pl.ds(pl.multiple_of((g * LOCAL_GROUP + i) * HD, HD), HD)
                for i in range(LOCAL_GROUP)
            ]
            scores = [
                (dot(lq[:, at], tails[0, :, at], ((1,), (1,))), dot(lq[:, at], lk[:, at], ((1,), (1,))))
                for at in ats
            ]
            parts = []
            for before, own in scores:
                before = jnp.where(window, before * SCALE, LOW)
                own = jnp.where(causal, own * SCALE, LOW)
                top = jnp.max(jnp.maximum(before, own), axis=1, keepdims=True)
                before, own = jnp.exp2(before - top), jnp.exp2(own - top)
                total = jnp.sum(before + own, axis=1, keepdims=True)
                parts.append((before.astype(BF16), own.astype(BF16), total))
            mixed = [
                (dot(before, tails[1, :, at]) + dot(own, lv[:, at])) / total
                for at, (before, own, total) in zip(ats, parts)
            ]
            for at, mix in zip(ats, mixed):
                lout[:, at] = mix.astype(BF16)

        local_copy(half).start()

    for load in loads:
        load.wait()
    local_heads(0)

    @pl.when(core == 1)
    def _():
        local_heads(1)

    await_sends(bulk_send.at[0], vbuf)
    @pl.when(core == 1)
    def _():
        start_tails(1)
    spread(head_block(value), vbuf.at[t], bulk_send.at[2], v_recv.at[z])


    @pl.when(is_owner)
    def _():
        def paired(a, b):
            width = a.shape[1]
            return jnp.concatenate(
                [a.reshape(CLUSTERS, MOST, width), b.reshape(CLUSTERS, MOST, width)], axis=1
            ).astype(BF16)

        def pair_at(i):
            return pl.ds(pl.multiple_of(i * 2 * MOST, 2 * MOST), 2 * MOST)

        def expand(buf, recv, target):
            @pl.loop(0, 8)
            def _(i):
                ahead = jnp.where(i % 2 == 1, (i + 1) // 2, 8 - i // 2)
                at_z = (z + ahead) % 8
                group = buf.at[pl.ds(0, 8)]
                pltpu.make_async_copy(group, group, recv.at[at_z]).wait()
                sources = [at_y * 16 + at_z * 2 + c for at_y in range(4) for c in range(2)]
                products = [dot(hot[d], buf[d]) for d in sources]
                for at_y in range(4):
                    target[:, pair_at(at_y * 8 + at_z), :] = paired(
                        products[2 * at_y], products[2 * at_y + 1]
                    )

        expand(qbuf, q_recv, qe)
        pl.semaphore_signal(ready, inc=1, device_id=(prev_s, t), device_id_type=MESH)
        expand(kbuf, k_recv, ke)

        stored = (weights0, weights1, weights2, weights3)
        for part in range(PARTS):
            lo, hi = part * TOK, (part + 1) * TOK

            def soften(scores, c):
                row0, row1 = bias0[c, :, :hi], bias1[c, :, :hi]
                later = rows_at.astype(F32) + lo >= split[c]
                tiles = []
                for j in range(part + 1):
                    cut = slice(j * TOK, (j + 1) * TOK)
                    bias = row0[:, cut]
                    if part >= BLOCK // TOK:
                        bias = jnp.where(later, row1[:, cut], bias)
                    tile = scores[:, cut] * SCALE + bias
                    if j == part:
                        tile = jnp.where(causal, tile, LOW)
                    tiles.append(tile)
                top = jnp.max(functools.reduce(jnp.maximum, tiles), axis=1, keepdims=True)
                return jnp.concatenate([jnp.exp2(tile - top).astype(BF16) for tile in tiles], axis=1)

            @pl.loop(0, CLUSTERS // GROUPS[part])
            def _(g):
                clusters = [g * GROUPS[part] + i for i in range(GROUPS[part])]
                scores = [dot(qe[c, lo:hi, :], ke[c, 0:hi, :], ((1,), (1,))) for c in clusters]
                weights = [soften(score, c) for score, c in zip(scores, clusters)]
                for c, weight in zip(clusters, weights):
                    stored[part][c] = weight

        expand(vbuf, v_recv, ke)
        pl.semaphore_wait(ready, 1)
        ones = jnp.ones((SLOTS, HD), BF16)
        for part in range(PARTS):
            lo, hi = part * TOK, (part + 1) * TOK

            @pl.loop(0, CLUSTERS // GROUPS[part])
            def _(g):
                clusters = [g * GROUPS[part] + i for i in range(GROUPS[part])]
                mixed = []
                for c in clusters:
                    operand = jnp.concatenate([ke[c, 0:hi, :], ones[:hi]], axis=1)
                    product = dot(stored[part][c], operand)
                    mixed.append((product[:, :HD] / product[:, HD:]).astype(BF16))
                for c, mix in zip(clusters, mixed):
                    qe[c, lo:hi, :] = mix

            @pl.loop(part * 2, part * 2 + 2)
            def _(g):
                sums = []
                for i in range(4):
                    rows = qe[:, pair_at(g * 4 + i), :].astype(F32)
                    for side in range(2):
                        slot_rows = rows[:, side * MOST : (side + 1) * MOST, :]
                        slot_rows = slot_rows.reshape(SLOTS, HD).astype(BF16)
                        sums.append(dot(hot[g * 8 + 2 * i + side], slot_rows, ((0,), (0,))).astype(BF16))
                for i in range(8):
                    vbuf[g * 8 + i] = sums[i]
                for i in range(8):
                    pltpu.make_async_remote_copy(
                        src_ref=vbuf.at[g * 8 + i],
                        dst_ref=out.at[:, pl.ds(pl.multiple_of(HALF + head * HD, HD), HD)],
                        send_sem=back_send, recv_sem=out_recv,
                        device_id=(next_s, g * 8 + i), device_id_type=MESH,
                    ).start()

        pltpu.make_async_copy(vbuf, vbuf, back_send).wait()

    @pl.when(core == 0)
    def _():
        local_heads(1)

    for half in range(2):
        local_copy(half).wait_send()
        for copy in tail_copies(half):
            copy.wait_send()
    await_sends(meta_send, meta)
    await_sends(bulk_send.at[1], vbuf)
    await_sends(bulk_send.at[2], vbuf)
    pltpu.make_async_copy(out, out, out_recv).wait()


def on_device(queries, keys, values, cluster_ids):
    any_space = pl.BlockSpec(memory_space=pl.ANY)
    vmem = pltpu.VMEM
    expanded = vmem((CLUSTERS, SLOTS, HD), BF16)
    wide = vmem((TOK, HALF), BF16)
    dma = pltpu.SemaphoreType.DMA
    layer = pl.pallas_call(
        layer_kernel,
        out_shape=jax.ShapeDtypeStruct((TOK, 2 * HALF), BF16),
        in_specs=[any_space] * 3 + [pl.BlockSpec(memory_space=vmem)],
        out_specs=any_space,
        scratch_shapes=[
            vmem((PEERS, 8, TOK), jnp.int32),
            vmem((8, TOK), jnp.int32),
            vmem((PEERS, TOK, HD), BF16),
            vmem((PEERS, TOK, HD), BF16),
            vmem((PEERS, TOK, HD), BF16),
            vmem((PEERS, SLOTS, TOK), BF16),
            expanded, expanded,
            *(vmem((CLUSTERS, TOK, (part + 1) * TOK), BF16) for part in range(PARTS)),
            vmem((CLUSTERS, 1, SLOTS), F32),
            vmem((CLUSTERS, 1, SLOTS), F32),
            vmem((CLUSTERS, 1, TOK), F32),
            wide, wide, wide,
            vmem((2, TOK, HALF), BF16),
            wide,
            dma, dma, dma((3,)), dma((8,)), dma((8,)), dma((8,)), dma((2, 2)), dma((2, 2)),
            dma((3,)), dma((2,)), dma, dma, pltpu.SemaphoreType.REGULAR,
        ],
        compiler_params=pltpu.CompilerParams(
            collective_id=0, has_side_effects=True, vmem_limit_bytes=60 << 20
        ),
    )(queries[0], keys[0], values[0], cluster_ids[0].T)
    return layer[None]


def solution(mesh):
    spec = P("section", "tok", None)
    return jax.shard_map(
        on_device, mesh=mesh, in_specs=(spec,) * 4, out_specs=spec, check_vma=False
    )
```

```python
import functools
import math

import jax
import jax.numpy as jnp
from jax import lax
from jax.experimental import pallas as pl
from jax.experimental.pallas import tpu as pltpu
from jax.sharding import PartitionSpec as P

HD = 128
TOK = 128
HEADS = 20
HALF = HEADS * HD
PEERS = 64
CLUSTERS = 64
MOST = 8
LOCAL_GROUP = 5
SLOTS = PEERS * MOST
PARTS = SLOTS // TOK
GROUPS = (16, 16, 8, 8)
BLOCK = 256
LOW = -1e30
SCALE = math.log2(math.e) / math.sqrt(HD)
MESH = pl.DeviceIdType.MESH
BF16 = jnp.bfloat16
F32 = jnp.float32


def owner_of(head):
    pair = head // 5
    within = head % 5
    z = pair * 2 + within // 3
    y = head % 4
    return (y * 8 + z) * 2 + 1


def iota(shape, dim):
    return lax.broadcasted_iota(jnp.int32, shape, dim)


def dot(a, b, dims=((1,), (0,))):
    return lax.dot_general(a, b, (dims, ((), ())), preferred_element_type=F32)


def one_hot(hit):
    return jnp.where(hit, 1.0, 0.0).astype(BF16)


def layer_kernel(
    query, key, value, ids, out,
    meta, slots, qbuf, kbuf, vbuf, hot, qe, ke, weights0, weights1, weights2, weights3,
    bias0, bias1, split, lq, lk, lv, tails, guest, stats, lout,
    meta_send, meta_recv, bulk_send, q_recv, k_recv, v_recv, tail_send, tail_recv, guest_send, guest_recv,
    load_sem, lout_send, back_send, out_recv, ready,
):
    s = lax.axis_index("section")
    t = lax.axis_index("tok")
    y, z, core = t // 16, (t // 2) % 8, t % 2
    first = (z // 2) * 5 + (z % 2) * 3
    offset = (y - first + 64) % 4
    head = first + offset
    is_owner = jnp.logical_and(offset < 3 - z % 2, core == 1)
    next_t, prev_t = (t + 1) % PEERS, (t + PEERS - 1) % PEERS
    next_s, prev_s = (s + 1) % 4, (s + 3) % 4

    barrier = pltpu.get_barrier_semaphore()

    @pl.when(is_owner)
    def _():
        @pl.loop(1, PEERS)
        def _(j):
            pl.semaphore_signal(
                barrier, inc=1, device_id=(s, (t + j) % PEERS), device_id_type=MESH
            )

    for peer in ((s, prev_t), (s, next_t), (prev_s, t), (next_s, t)):
        pl.semaphore_signal(barrier, inc=1, device_id=peer, device_id_type=MESH)

    slots[...] = jnp.zeros_like(slots)
    rows_at, cols_at = iota((TOK, TOK), 0), iota((TOK, TOK), 1)
    eye = rows_at == cols_at
    earlier = rows_at < cols_at
    picks = [ids[j : j + 1, :] for j in range(2)]
    col0, col1 = [jnp.sum(jnp.where(eye, row, 0), axis=1, keepdims=True) for row in picks]
    for j, row in enumerate(picks):
        same = jnp.logical_and(earlier, jnp.logical_or(col0 == row, col1 == row))
        rank = jnp.sum(jnp.where(same, 1, 0), axis=0, keepdims=True)
        slots[j : j + 1, :] = row * MOST + rank
    named = jnp.logical_or(col0 == cols_at, col1 == cols_at)
    slots[2:3, :] = jnp.sum(jnp.where(named, 1, 0), axis=0, keepdims=True)

    loads = [
        pltpu.make_async_copy(src.at[:, pl.ds(0, HALF)], dst, load_sem.at[a])
        for a, (src, dst) in enumerate(((query, lq), (key, lk), (value, lv)))
    ]
    for load in loads:
        load.start()

    pl.semaphore_wait(barrier, jnp.where(is_owner, HEADS - 1, HEADS) + 4)

    def spread(source, target, send, recv):
        @pl.loop(0, HEADS)
        def _(i):
            step = jnp.where(i % 2 == 0, i // 2, HEADS - 1 - i // 2)
            h = (first + step) % HEADS
            owner = owner_of(h)

            @pl.when(owner != t)
            def _():
                pltpu.make_async_remote_copy(
                    src_ref=source(h), dst_ref=target, send_sem=send, recv_sem=recv,
                    device_id=(s, owner), device_id_type=MESH,
                ).start()

            @pl.when(owner == t)
            def _():
                pltpu.make_async_copy(source(h), target, recv).start()

    def head_block(array):
        return lambda h: array.at[:, pl.ds(pl.multiple_of(HALF + h * HD, HD), HD)]

    tail_copies = [
        pltpu.make_async_remote_copy(
            src_ref=src.at[:, pl.ds(0, HALF)], dst_ref=tails.at[a],
            send_sem=tail_send.at[a], recv_sem=tail_recv.at[a],
            device_id=(s, next_t), device_id_type=MESH,
        )
        for a, src in enumerate((key, value))
    ]
    visit = pltpu.make_async_remote_copy(
        src_ref=query.at[:, pl.ds(0, HALF)], dst_ref=guest,
        send_sem=guest_send.at[0], recv_sem=guest_recv.at[0],
        device_id=(s, prev_t), device_id_type=MESH,
    )
    returns = [
        pltpu.make_async_remote_copy(
            src_ref=src, dst_ref=dst, send_sem=guest_send.at[a], recv_sem=guest_recv.at[a],
            device_id=(s, next_t), device_id_type=MESH,
        )
        for a, (src, dst) in enumerate(((guest, tails.at[0]), (stats.at[0], stats.at[1])), 1)
    ]

    spread(lambda h: slots, meta.at[t], meta_send, meta_recv)

    @pl.when(core == 0)
    def _():
        visit.start()
        for copy in tail_copies:
            copy.start()

    spread(head_block(query), qbuf.at[t], bulk_send.at[0], q_recv.at[z])
    spread(head_block(key), kbuf.at[t], bulk_send.at[1], k_recv.at[z])

    def await_sends(sem, buf):
        for many, mine in ((HEADS - 1, True), (HEADS, False)):

            @pl.when(is_owner if mine else jnp.logical_not(is_owner))
            def _():
                ref = buf.at[pl.ds(0, many)]
                pltpu.make_async_copy(ref, ref, sem).wait()

    @pl.when(is_owner)
    def _():
        pltpu.make_async_copy(meta, meta, meta_recv).wait()
        counts = meta[:, 2, :].astype(F32).astype(BF16)
        dev = iota((PEERS, SLOTS), 0)
        of_dev = iota((PEERS, SLOTS), 1) // MOST
        count = dot(counts, one_hot(dev == of_dev), ((0,), (0,)))
        before = dot(counts, one_hot(dev < of_dev), ((0,), (0,)))
        place = (iota((TOK, SLOTS), 1) % MOST).astype(F32)
        filled = place < count
        second = before + jnp.minimum(place, count) >= BLOCK
        def by_cluster(array):
            return array[:CLUSTERS].reshape(CLUSTERS, 1, array.shape[1])

        slot_at = iota((SLOTS, TOK), 0)

        @pl.loop(0, PEERS // 4)
        def _(g):
            for i in range(4):
                d = g * 4 + i
                hot[d] = one_hot(
                    jnp.logical_or(slot_at == meta[d, 0:1, :], slot_at == meta[d, 1:2, :])
                )

        bias0[...] = by_cluster(jnp.where(filled, 0.0, LOW))
        bias1[...] = by_cluster(jnp.where(jnp.logical_and(filled, second), 0.0, LOW))
        start = jnp.sum(jnp.where(second, 0.0, 1.0), axis=1, keepdims=True)
        split[...] = by_cluster(jnp.broadcast_to(start, (TOK, TOK)))

    window = cols_at > rows_at
    causal = cols_at <= rows_at
    local_copy = pltpu.make_async_remote_copy(
        src_ref=lout, dst_ref=out.at[:, pl.ds(0, HALF)], send_sem=lout_send, recv_sem=out_recv,
        device_id=(next_s, t), device_id_type=MESH,
    )

    def heads_at(g):
        heads = [g * LOCAL_GROUP + i for i in range(LOCAL_GROUP)]
        return [(h, pl.ds(pl.multiple_of(h * HD, HD), HD)) for h in heads]

    def soft(scores, mask):
        scores = jnp.where(mask, scores * SCALE, LOW)
        top = jnp.max(scores, axis=1, keepdims=True)
        weights = jnp.exp2(scores - top)
        return weights.astype(BF16), top, jnp.sum(weights, axis=1, keepdims=True)

    for load in loads:
        load.wait()

    @pl.when(core == 1)
    def _():
        visit.wait_recv()

        def host(g, noted):
            group = heads_at(g)
            scores = [dot(guest[:, at], lk[:, at], ((1,), (1,))) for _, at in group]
            parts = [soft(score, window) for score in scores]
            mixed = [dot(part[0], lv[:, at]) / part[2] for part, (_, at) in zip(parts, group)]
            for (h, at), (_, top, total), mix in zip(group, parts, mixed):
                guest[:, at] = mix.astype(BF16)
                noted = jnp.where(cols_at == h, top, noted)
                noted = jnp.where(cols_at == TOK // 2 + h, total, noted)
            return noted

        stats[0] = lax.fori_loop(0, HEADS // LOCAL_GROUP, host, jnp.zeros((TOK, TOK), F32))
        for copy in returns:
            copy.start()
        for copy in tail_copies:
            copy.wait_recv()

        @pl.loop(0, HEADS // LOCAL_GROUP)
        def _(g):
            group = heads_at(g)
            scores = [
                (dot(lq[:, at], tails[0, :, at], ((1,), (1,))), dot(lq[:, at], lk[:, at], ((1,), (1,))))
                for _, at in group
            ]
            parts = []
            for before, own in scores:
                before = jnp.where(window, before * SCALE, LOW)
                own = jnp.where(causal, own * SCALE, LOW)
                top = jnp.max(jnp.maximum(before, own), axis=1, keepdims=True)
                before, own = jnp.exp2(before - top), jnp.exp2(own - top)
                total = jnp.sum(before + own, axis=1, keepdims=True)
                parts.append((before.astype(BF16), own.astype(BF16), total))
            mixed = [
                (dot(before, tails[1, :, at]) + dot(own, lv[:, at])) / total
                for (_, at), (before, own, total) in zip(group, parts)
            ]
            for (_, at), mix in zip(group, mixed):
                lout[:, at] = mix.astype(BF16)

        local_copy.start()

    await_sends(bulk_send.at[0], vbuf)
    spread(head_block(value), vbuf.at[t], bulk_send.at[2], v_recv.at[z])


    @pl.when(core == 0)
    def _():
        for copy in returns:
            copy.wait_recv()
        noted = stats[1]

        @pl.loop(0, HEADS // LOCAL_GROUP)
        def _(g):
            group = heads_at(g)
            scores = [dot(lq[:, at], lk[:, at], ((1,), (1,))) for _, at in group]
            parts = [soft(score, causal) for score in scores]
            mixed = [dot(part[0], lv[:, at]) for part, (_, at) in zip(parts, group)]
            for (h, at), (_, top, total), mix in zip(group, parts, mixed):
                before_top = jnp.sum(jnp.where(cols_at == h, noted, 0.0), axis=1, keepdims=True)
                before_top = jnp.where(t == 0, LOW, before_top)
                before_total = jnp.sum(
                    jnp.where(cols_at == TOK // 2 + h, noted, 0.0), axis=1, keepdims=True
                )
                highest = jnp.maximum(top, before_top)
                before = jnp.exp2(before_top - highest) * before_total
                own = jnp.exp2(top - highest)
                both = before * tails[0, :, at].astype(F32) + own * mix
                lout[:, at] = (both / (before + own * total)).astype(BF16)

        local_copy.start()

    @pl.when(is_owner)
    def _():
        def paired(a, b):
            width = a.shape[1]
            return jnp.concatenate(
                [a.reshape(CLUSTERS, MOST, width), b.reshape(CLUSTERS, MOST, width)], axis=1
            ).astype(BF16)

        def pair_at(i):
            return pl.ds(pl.multiple_of(i * 2 * MOST, 2 * MOST), 2 * MOST)

        def expand(buf, recv, target):
            @pl.loop(0, 8)
            def _(i):
                ahead = jnp.where(i % 2 == 1, (i + 1) // 2, 8 - i // 2)
                at_z = (z + ahead) % 8
                group = buf.at[pl.ds(0, 8)]
                pltpu.make_async_copy(group, group, recv.at[at_z]).wait()
                sources = [at_y * 16 + at_z * 2 + c for at_y in range(4) for c in range(2)]
                products = [dot(hot[d], buf[d]) for d in sources]
                for at_y in range(4):
                    target[:, pair_at(at_y * 8 + at_z), :] = paired(
                        products[2 * at_y], products[2 * at_y + 1]
                    )

        expand(qbuf, q_recv, qe)
        pl.semaphore_signal(ready, inc=1, device_id=(prev_s, t), device_id_type=MESH)
        expand(kbuf, k_recv, ke)

        stored = (weights0, weights1, weights2, weights3)
        for part in range(PARTS):
            lo, hi = part * TOK, (part + 1) * TOK

            def soften(scores, c):
                row0, row1 = bias0[c, :, :hi], bias1[c, :, :hi]
                later = rows_at.astype(F32) + lo >= split[c]
                tiles = []
                for j in range(part + 1):
                    cut = slice(j * TOK, (j + 1) * TOK)
                    bias = row0[:, cut]
                    if part >= BLOCK // TOK:
                        bias = jnp.where(later, row1[:, cut], bias)
                    tile = scores[:, cut] * SCALE + bias
                    if j == part:
                        tile = jnp.where(causal, tile, LOW)
                    tiles.append(tile)
                top = jnp.max(functools.reduce(jnp.maximum, tiles), axis=1, keepdims=True)
                return jnp.concatenate([jnp.exp2(tile - top).astype(BF16) for tile in tiles], axis=1)

            @pl.loop(0, CLUSTERS // GROUPS[part])
            def _(g):
                clusters = [g * GROUPS[part] + i for i in range(GROUPS[part])]
                scores = [dot(qe[c, lo:hi, :], ke[c, 0:hi, :], ((1,), (1,))) for c in clusters]
                weights = [soften(score, c) for score, c in zip(scores, clusters)]
                for c, weight in zip(clusters, weights):
                    stored[part][c] = weight

        expand(vbuf, v_recv, ke)
        pl.semaphore_wait(ready, 1)
        ones = jnp.ones((SLOTS, HD), BF16)
        for part in range(PARTS):
            lo, hi = part * TOK, (part + 1) * TOK

            @pl.loop(0, CLUSTERS // GROUPS[part])
            def _(g):
                clusters = [g * GROUPS[part] + i for i in range(GROUPS[part])]
                mixed = []
                for c in clusters:
                    operand = jnp.concatenate([ke[c, 0:hi, :], ones[:hi]], axis=1)
                    product = dot(stored[part][c], operand)
                    mixed.append((product[:, :HD] / product[:, HD:]).astype(BF16))
                for c, mix in zip(clusters, mixed):
                    qe[c, lo:hi, :] = mix

            @pl.loop(part * 2, part * 2 + 2)
            def _(g):
                sums = []
                for i in range(4):
                    rows = qe[:, pair_at(g * 4 + i), :].astype(F32)
                    for side in range(2):
                        slot_rows = rows[:, side * MOST : (side + 1) * MOST, :]
                        slot_rows = slot_rows.reshape(SLOTS, HD).astype(BF16)
                        sums.append(dot(hot[g * 8 + 2 * i + side], slot_rows, ((0,), (0,))).astype(BF16))
                for i in range(8):
                    vbuf[g * 8 + i] = sums[i]
                for i in range(8):
                    pltpu.make_async_remote_copy(
                        src_ref=vbuf.at[g * 8 + i],
                        dst_ref=out.at[:, pl.ds(pl.multiple_of(HALF + head * HD, HD), HD)],
                        send_sem=back_send, recv_sem=out_recv,
                        device_id=(next_s, g * 8 + i), device_id_type=MESH,
                    ).start()

        pltpu.make_async_copy(vbuf, vbuf, back_send).wait()

    local_copy.wait_send()

    @pl.when(core == 0)
    def _():
        visit.wait_send()
        for copy in tail_copies:
            copy.wait_send()

    @pl.when(core == 1)
    def _():
        for copy in returns:
            copy.wait_send()

    await_sends(meta_send, meta)
    await_sends(bulk_send.at[1], vbuf)
    await_sends(bulk_send.at[2], vbuf)
    pltpu.make_async_copy(out, out, out_recv).wait()


def on_device(queries, keys, values, cluster_ids):
    any_space = pl.BlockSpec(memory_space=pl.ANY)
    vmem = pltpu.VMEM
    expanded = vmem((CLUSTERS, SLOTS, HD), BF16)
    wide = vmem((TOK, HALF), BF16)
    dma = pltpu.SemaphoreType.DMA
    layer = pl.pallas_call(
        layer_kernel,
        out_shape=jax.ShapeDtypeStruct((TOK, 2 * HALF), BF16),
        in_specs=[any_space] * 3 + [pl.BlockSpec(memory_space=vmem)],
        out_specs=any_space,
        scratch_shapes=[
            vmem((PEERS, 8, TOK), jnp.int32),
            vmem((8, TOK), jnp.int32),
            vmem((PEERS, TOK, HD), BF16),
            vmem((PEERS, TOK, HD), BF16),
            vmem((PEERS, TOK, HD), BF16),
            vmem((PEERS, SLOTS, TOK), BF16),
            expanded, expanded,
            *(vmem((CLUSTERS, TOK, (part + 1) * TOK), BF16) for part in range(PARTS)),
            vmem((CLUSTERS, 1, SLOTS), F32),
            vmem((CLUSTERS, 1, SLOTS), F32),
            vmem((CLUSTERS, 1, TOK), F32),
            wide, wide, wide,
            vmem((2, TOK, HALF), BF16),
            wide,
            vmem((2, TOK, TOK), F32),
            wide,
            dma, dma, dma((3,)), dma((8,)), dma((8,)), dma((8,)), dma((2,)), dma((2,)), dma((3,)), dma((3,)),
            dma((3,)), dma, dma, dma, pltpu.SemaphoreType.REGULAR,
        ],
        compiler_params=pltpu.CompilerParams(
            collective_id=0, has_side_effects=True, vmem_limit_bytes=60 << 20
        ),
    )(queries[0], keys[0], values[0], cluster_ids[0].T)
    return layer[None]


def solution(mesh):
    spec = P("section", "tok", None)
    return jax.shard_map(
        on_device, mesh=mesh, in_specs=(spec,) * 4, out_specs=spec, check_vma=False
    )
```

```python
import functools
import math

import jax
import jax.numpy as jnp
from jax import lax
from jax.experimental import pallas as pl
from jax.experimental.pallas import tpu as pltpu
from jax.sharding import PartitionSpec as P

HD = 128
TOK = 128
HEADS = 20
HALF = HEADS * HD
PEERS = 64
CLUSTERS = 64
MOST = 8
LOCAL_GROUP = 5
SLOTS = PEERS * MOST
PARTS = SLOTS // TOK
GROUPS = (16, 16, 8, 8)
BLOCK = 256
LOW = -1e30
SCALE = math.log2(math.e) / math.sqrt(HD)
MESH = pl.DeviceIdType.MESH
BF16 = jnp.bfloat16
F32 = jnp.float32


def owner_of(head):
    pair = head // 5
    within = head % 5
    z = pair * 2 + within // 3
    y = head % 4
    return (y * 8 + z) * 2 + 1


def iota(shape, dim):
    return lax.broadcasted_iota(jnp.int32, shape, dim)


def dot(a, b, dims=((1,), (0,))):
    return lax.dot_general(a, b, (dims, ((), ())), preferred_element_type=F32)


def one_hot(hit):
    return jnp.where(hit, 1.0, 0.0).astype(BF16)


def layer_kernel(
    query, key, value, ids, out,
    meta, slots, qbuf, kbuf, vbuf, hot, qe, ke, weights0, weights1, weights2, weights3,
    bias0, bias1, split, lq, lk, lv, tails, guest, stats, lout,
    meta_send, meta_recv, bulk_send, q_recv, k_recv, v_recv, tail_send, tail_recv, guest_send, guest_recv,
    load_sem, lout_send, back_send, out_recv, ready,
):
    s = lax.axis_index("section")
    t = lax.axis_index("tok")
    y, z, core = t // 16, (t // 2) % 8, t % 2
    first = (z // 2) * 5 + (z % 2) * 3
    offset = (y - first + 64) % 4
    head = first + offset
    is_owner = jnp.logical_and(offset < 3 - z % 2, core == 1)
    next_t, prev_t = (t + 1) % PEERS, (t + PEERS - 1) % PEERS
    next_s, prev_s = (s + 1) % 4, (s + 3) % 4

    barrier = pltpu.get_barrier_semaphore()

    @pl.when(is_owner)
    def _():
        @pl.loop(1, PEERS)
        def _(j):
            pl.semaphore_signal(
                barrier, inc=1, device_id=(s, (t + j) % PEERS), device_id_type=MESH
            )

    for peer in ((s, prev_t), (s, next_t), (prev_s, t), (next_s, t)):
        pl.semaphore_signal(barrier, inc=1, device_id=peer, device_id_type=MESH)

    slots[...] = jnp.zeros_like(slots)
    rows_at, cols_at = iota((TOK, TOK), 0), iota((TOK, TOK), 1)
    eye = rows_at == cols_at
    earlier = rows_at < cols_at
    picks = [ids[j : j + 1, :] for j in range(2)]
    col0, col1 = [jnp.sum(jnp.where(eye, row, 0), axis=1, keepdims=True) for row in picks]
    for j, row in enumerate(picks):
        same = jnp.logical_and(earlier, jnp.logical_or(col0 == row, col1 == row))
        rank = jnp.sum(jnp.where(same, 1, 0), axis=0, keepdims=True)
        slots[j : j + 1, :] = row * MOST + rank
    named = jnp.logical_or(col0 == cols_at, col1 == cols_at)
    slots[2:3, :] = jnp.sum(jnp.where(named, 1, 0), axis=0, keepdims=True)

    loads = [
        pltpu.make_async_copy(src.at[:, pl.ds(0, HALF)], dst, load_sem.at[a])
        for a, (src, dst) in enumerate(((query, lq), (key, lk), (value, lv)))
    ]
    for load in loads:
        load.start()

    pl.semaphore_wait(barrier, jnp.where(is_owner, HEADS - 1, HEADS) + 4)

    def spread(source, target, send, recv):
        @pl.loop(0, HEADS)
        def _(i):
            step = jnp.where(i % 2 == 0, i // 2, HEADS - 1 - i // 2)
            h = (first + step) % HEADS
            owner = owner_of(h)

            @pl.when(owner != t)
            def _():
                pltpu.make_async_remote_copy(
                    src_ref=source(h), dst_ref=target, send_sem=send, recv_sem=recv,
                    device_id=(s, owner), device_id_type=MESH,
                ).start()

            @pl.when(owner == t)
            def _():
                pltpu.make_async_copy(source(h), target, recv).start()

    def head_block(array):
        return lambda h: array.at[:, pl.ds(pl.multiple_of(HALF + h * HD, HD), HD)]

    tail_copies = [
        pltpu.make_async_remote_copy(
            src_ref=src.at[:, pl.ds(0, HALF)], dst_ref=tails.at[a],
            send_sem=tail_send.at[a], recv_sem=tail_recv.at[a],
            device_id=(s, next_t), device_id_type=MESH,
        )
        for a, src in enumerate((key, value))
    ]
    visit = pltpu.make_async_remote_copy(
        src_ref=query.at[:, pl.ds(0, HALF)], dst_ref=guest,
        send_sem=guest_send.at[0], recv_sem=guest_recv.at[0],
        device_id=(s, prev_t), device_id_type=MESH,
    )
    returns = [
        pltpu.make_async_remote_copy(
            src_ref=src, dst_ref=dst, send_sem=guest_send.at[a], recv_sem=guest_recv.at[a],
            device_id=(s, next_t), device_id_type=MESH,
        )
        for a, (src, dst) in enumerate(((guest, tails.at[0]), (stats.at[0], stats.at[1])), 1)
    ]

    spread(lambda h: slots, meta.at[t], meta_send, meta_recv)

    @pl.when(core == 0)
    def _():
        visit.start()
        for copy in tail_copies:
            copy.start()

    spread(head_block(query), qbuf.at[t], bulk_send.at[0], q_recv.at[z])
    spread(head_block(key), kbuf.at[t], bulk_send.at[1], k_recv.at[z])

    def await_sends(sem, buf):
        for many, mine in ((HEADS - 1, True), (HEADS, False)):

            @pl.when(is_owner if mine else jnp.logical_not(is_owner))
            def _():
                ref = buf.at[pl.ds(0, many)]
                pltpu.make_async_copy(ref, ref, sem).wait()

    @pl.when(is_owner)
    def _():
        pltpu.make_async_copy(meta, meta, meta_recv).wait()
        counts = meta[:, 2, :].astype(F32).astype(BF16)
        dev = iota((PEERS, SLOTS), 0)
        of_dev = iota((PEERS, SLOTS), 1) // MOST
        count = dot(counts, one_hot(dev == of_dev), ((0,), (0,)))
        before = dot(counts, one_hot(dev < of_dev), ((0,), (0,)))
        place = (iota((TOK, SLOTS), 1) % MOST).astype(F32)
        filled = place < count
        second = before + jnp.minimum(place, count) >= BLOCK
        def by_cluster(array):
            return array[:CLUSTERS].reshape(CLUSTERS, 1, array.shape[1])

        slot_at = iota((SLOTS, TOK), 0)

        @pl.loop(0, PEERS // 4)
        def _(g):
            for i in range(4):
                d = g * 4 + i
                hot[d] = one_hot(
                    jnp.logical_or(slot_at == meta[d, 0:1, :], slot_at == meta[d, 1:2, :])
                )

        bias0[...] = by_cluster(jnp.where(filled, 0.0, LOW))
        bias1[...] = by_cluster(jnp.where(jnp.logical_and(filled, second), 0.0, LOW))
        start = jnp.sum(jnp.where(second, 0.0, 1.0), axis=1, keepdims=True)
        split[...] = by_cluster(jnp.broadcast_to(start, (TOK, TOK)))

    window = cols_at > rows_at
    causal = cols_at <= rows_at
    local_copy = pltpu.make_async_remote_copy(
        src_ref=lout, dst_ref=out.at[:, pl.ds(0, HALF)], send_sem=lout_send, recv_sem=out_recv,
        device_id=(next_s, t), device_id_type=MESH,
    )

    def heads_at(g):
        heads = [g * LOCAL_GROUP + i for i in range(LOCAL_GROUP)]
        return [(h, pl.ds(pl.multiple_of(h * HD, HD), HD)) for h in heads]

    def soft(scores, mask):
        scores = jnp.where(mask, scores * SCALE, LOW)
        top = jnp.max(scores, axis=1, keepdims=True)
        weights = jnp.exp2(scores - top)
        return weights.astype(BF16), top, jnp.sum(weights, axis=1, keepdims=True)

    for load in loads:
        load.wait()

    @pl.when(core == 1)
    def _():
        visit.wait_recv()

        def host(g, noted):
            group = heads_at(g)
            scores = [dot(guest[:, at], lk[:, at], ((1,), (1,))) for _, at in group]
            parts = [soft(score, window) for score in scores]
            mixed = [dot(part[0], lv[:, at]) / part[2] for part, (_, at) in zip(parts, group)]
            for (h, at), (_, top, total), mix in zip(group, parts, mixed):
                guest[:, at] = mix.astype(BF16)
                noted = jnp.where(cols_at == h, top, noted)
                noted = jnp.where(cols_at == TOK // 2 + h, total, noted)
            return noted

        stats[0] = lax.fori_loop(0, HEADS // LOCAL_GROUP, host, jnp.zeros((TOK, TOK), F32))
        for copy in returns:
            copy.start()
        for copy in tail_copies:
            copy.wait_recv()

        @pl.loop(0, HEADS // LOCAL_GROUP)
        def _(g):
            group = heads_at(g)
            scores = [
                (dot(lq[:, at], tails[0, :, at], ((1,), (1,))), dot(lq[:, at], lk[:, at], ((1,), (1,))))
                for _, at in group
            ]
            parts = []
            for before, own in scores:
                before = jnp.where(window, before * SCALE, LOW)
                own = jnp.where(causal, own * SCALE, LOW)
                top = jnp.max(jnp.maximum(before, own), axis=1, keepdims=True)
                before, own = jnp.exp2(before - top), jnp.exp2(own - top)
                total = jnp.sum(before + own, axis=1, keepdims=True)
                parts.append((before.astype(BF16), own.astype(BF16), total))
            mixed = [
                (dot(before, tails[1, :, at]) + dot(own, lv[:, at])) / total
                for (_, at), (before, own, total) in zip(group, parts)
            ]
            for (_, at), mix in zip(group, mixed):
                lout[:, at] = mix.astype(BF16)

        local_copy.start()

    spread(head_block(value), vbuf.at[t], bulk_send.at[2], v_recv.at[z])


    @pl.when(core == 0)
    def _():
        for copy in returns:
            copy.wait_recv()
        noted = stats[1]

        @pl.loop(0, HEADS // LOCAL_GROUP)
        def _(g):
            group = heads_at(g)
            scores = [dot(lq[:, at], lk[:, at], ((1,), (1,))) for _, at in group]
            parts = [soft(score, causal) for score in scores]
            mixed = [dot(part[0], lv[:, at]) for part, (_, at) in zip(parts, group)]
            for (h, at), (_, top, total), mix in zip(group, parts, mixed):
                before_top = jnp.sum(jnp.where(cols_at == h, noted, 0.0), axis=1, keepdims=True)
                before_top = jnp.where(t == 0, LOW, before_top)
                before_total = jnp.sum(
                    jnp.where(cols_at == TOK // 2 + h, noted, 0.0), axis=1, keepdims=True
                )
                highest = jnp.maximum(top, before_top)
                before = jnp.exp2(before_top - highest) * before_total
                own = jnp.exp2(top - highest)
                both = before * tails[0, :, at].astype(F32) + own * mix
                lout[:, at] = (both / (before + own * total)).astype(BF16)

        local_copy.start()

    @pl.when(is_owner)
    def _():
        def paired(a, b):
            width = a.shape[1]
            return jnp.concatenate(
                [a.reshape(CLUSTERS, MOST, width), b.reshape(CLUSTERS, MOST, width)], axis=1
            ).astype(BF16)

        def pair_at(i):
            return pl.ds(pl.multiple_of(i * 2 * MOST, 2 * MOST), 2 * MOST)

        def expand(buf, recv, target):
            @pl.loop(0, 8)
            def _(i):
                ahead = jnp.where(i % 2 == 1, (i + 1) // 2, 8 - i // 2)
                at_z = (z + ahead) % 8
                group = buf.at[pl.ds(0, 8)]
                pltpu.make_async_copy(group, group, recv.at[at_z]).wait()
                sources = [at_y * 16 + at_z * 2 + c for at_y in range(4) for c in range(2)]
                products = [dot(hot[d], buf[d]) for d in sources]
                for at_y in range(4):
                    target[:, pair_at(at_y * 8 + at_z), :] = paired(
                        products[2 * at_y], products[2 * at_y + 1]
                    )

        expand(qbuf, q_recv, qe)
        pl.semaphore_signal(ready, inc=1, device_id=(prev_s, t), device_id_type=MESH)
        expand(kbuf, k_recv, ke)

        stored = (weights0, weights1, weights2, weights3)
        for part in range(PARTS):
            lo, hi = part * TOK, (part + 1) * TOK

            def soften(scores, c):
                row0, row1 = bias0[c, :, :hi], bias1[c, :, :hi]
                later = rows_at.astype(F32) + lo >= split[c]
                tiles = []
                for j in range(part + 1):
                    cut = slice(j * TOK, (j + 1) * TOK)
                    bias = row0[:, cut]
                    if part >= BLOCK // TOK:
                        bias = jnp.where(later, row1[:, cut], bias)
                    tile = scores[:, cut] * SCALE + bias
                    if j == part:
                        tile = jnp.where(causal, tile, LOW)
                    tiles.append(tile)
                top = jnp.max(functools.reduce(jnp.maximum, tiles), axis=1, keepdims=True)
                return jnp.concatenate([jnp.exp2(tile - top).astype(BF16) for tile in tiles], axis=1)

            @pl.loop(0, CLUSTERS // GROUPS[part])
            def _(g):
                clusters = [g * GROUPS[part] + i for i in range(GROUPS[part])]
                scores = [dot(qe[c, lo:hi, :], ke[c, 0:hi, :], ((1,), (1,))) for c in clusters]
                weights = [soften(score, c) for score, c in zip(scores, clusters)]
                for c, weight in zip(clusters, weights):
                    stored[part][c] = weight

        expand(vbuf, v_recv, ke)
        pl.semaphore_wait(ready, 1)
        ones = jnp.ones((SLOTS, HD), BF16)
        for part in range(PARTS):
            lo, hi = part * TOK, (part + 1) * TOK

            @pl.loop(0, CLUSTERS // GROUPS[part])
            def _(g):
                clusters = [g * GROUPS[part] + i for i in range(GROUPS[part])]
                mixed = []
                for c in clusters:
                    operand = jnp.concatenate([ke[c, 0:hi, :], ones[:hi]], axis=1)
                    product = dot(stored[part][c], operand)
                    mixed.append((product[:, :HD] / product[:, HD:]).astype(BF16))
                for c, mix in zip(clusters, mixed):
                    qe[c, lo:hi, :] = mix

            @pl.loop(part * 2, part * 2 + 2)
            def _(g):
                sums = []
                for i in range(4):
                    rows = qe[:, pair_at(g * 4 + i), :].astype(F32)
                    for side in range(2):
                        slot_rows = rows[:, side * MOST : (side + 1) * MOST, :]
                        slot_rows = slot_rows.reshape(SLOTS, HD).astype(BF16)
                        sums.append(dot(hot[g * 8 + 2 * i + side], slot_rows, ((0,), (0,))).astype(BF16))
                for i in range(8):
                    vbuf[g * 8 + i] = sums[i]
                for i in range(8):
                    pltpu.make_async_remote_copy(
                        src_ref=vbuf.at[g * 8 + i],
                        dst_ref=out.at[:, pl.ds(pl.multiple_of(HALF + head * HD, HD), HD)],
                        send_sem=back_send, recv_sem=out_recv,
                        device_id=(next_s, g * 8 + i), device_id_type=MESH,
                    ).start()

        pltpu.make_async_copy(vbuf, vbuf, back_send).wait()

    local_copy.wait_send()

    @pl.when(core == 0)
    def _():
        visit.wait_send()
        for copy in tail_copies:
            copy.wait_send()

    @pl.when(core == 1)
    def _():
        for copy in returns:
            copy.wait_send()

    await_sends(meta_send, meta)
    await_sends(bulk_send.at[0], vbuf)
    await_sends(bulk_send.at[1], vbuf)
    await_sends(bulk_send.at[2], vbuf)
    pltpu.make_async_copy(out, out, out_recv).wait()


def on_device(queries, keys, values, cluster_ids):
    any_space = pl.BlockSpec(memory_space=pl.ANY)
    vmem = pltpu.VMEM
    expanded = vmem((CLUSTERS, SLOTS, HD), BF16)
    wide = vmem((TOK, HALF), BF16)
    dma = pltpu.SemaphoreType.DMA
    layer = pl.pallas_call(
        layer_kernel,
        out_shape=jax.ShapeDtypeStruct((TOK, 2 * HALF), BF16),
        in_specs=[any_space] * 3 + [pl.BlockSpec(memory_space=vmem)],
        out_specs=any_space,
        scratch_shapes=[
            vmem((PEERS, 8, TOK), jnp.int32),
            vmem((8, TOK), jnp.int32),
            vmem((PEERS, TOK, HD), BF16),
            vmem((PEERS, TOK, HD), BF16),
            vmem((PEERS, TOK, HD), BF16),
            vmem((PEERS, SLOTS, TOK), BF16),
            expanded, expanded,
            *(vmem((CLUSTERS, TOK, (part + 1) * TOK), BF16) for part in range(PARTS)),
            vmem((CLUSTERS, 1, SLOTS), F32),
            vmem((CLUSTERS, 1, SLOTS), F32),
            vmem((CLUSTERS, 1, TOK), F32),
            wide, wide, wide,
            vmem((2, TOK, HALF), BF16),
            wide,
            vmem((2, TOK, TOK), F32),
            wide,
            dma, dma, dma((3,)), dma((8,)), dma((8,)), dma((8,)), dma((2,)), dma((2,)), dma((3,)), dma((3,)),
            dma((3,)), dma, dma, dma, pltpu.SemaphoreType.REGULAR,
        ],
        compiler_params=pltpu.CompilerParams(
            collective_id=0, has_side_effects=True, vmem_limit_bytes=60 << 20
        ),
    )(queries[0], keys[0], values[0], cluster_ids[0].T)
    return layer[None]


def solution(mesh):
    spec = P("section", "tok", None)
    return jax.shard_map(
        on_device, mesh=mesh, in_specs=(spec,) * 4, out_specs=spec, check_vma=False
    )
```
